512 devices in a mesh: block: 4 (over y_hi, core), req: 16 (over x, y_lo), head: 8 (over z).
Axes of the slice: x: 4, y: 8 (y_hi: 2, y_lo: 4; y = y_hi * 4 + y_lo), z: 8, core: 2. Of those that a mesh axis runs over, the one named last changes fastest.
Arguments:
- tokens: bfloat16 [16, 4, 512, 3072], P('req', 'block', None, 'head'), may hold values from -400 to 400, as said below
- levels: int32 [16, 4], P('req', 'block'), may hold values from 0 to 31
- frames: int32 [16, 4], P('req'), may hold values from 1 to 8, as said below
- segment_mask: int32 [16, 4, 4], P('req'), may hold values 0 or 1
- mod_table: float32 [32, 2, 3072], replicated, may hold values from -3 to 3
- w_qkv: bfloat16 [3072, 9216], P('block', 'head'), may hold values from -0.109375 to 0.109375
- q_gain: float32 [128], replicated, may hold values from 0.1 to 1.9
- k_gain: float32 [128], replicated, may hold values from 0.1 to 1.9
Outputs:
- context: bfloat16 [16, 4, 512, 3072], P('req', 'block', None, 'head')
The draws below stay inside these ranges and needn't reach their ends.
Inputs may be any that keep to these rules, and one draw needn't show every extreme that they name: The first segment of every request holds all 8 frames. Hidden states of order one after the norm; individual tokens and features differ in scale.
All inputs are finite; a program needn't handle non-finite values. No bound on the sum of `segment_mask` on one device may be relied on, other than what follows from the above.
Results may differ from the reference program's by a relative error of at most 0.0042.
Values may be sent and summed in bfloat16 or wider, within the bound.
No kernel may reach another device: no remote copies, remote signals or barrier semaphores. Data moves between devices by JAX's collectives and lax.ppermute only.
A program may use at most 64 MiB of HBM per device.

```python
import math
import jax
import jax.numpy as jnp
from jax import lax

D = 3072
H = 24
HD = 128
LEVELS = 32
FRAMES = 8
TPF = 64
TOK = 512
SEGMENTS = 4
REQS = 16


def draw_tokens(key, part):
    key = jax.random.fold_in(key, 11)
    key_base, key_rows, key_cols = jax.random.split(key, 3)
    row_scale = jnp.exp(jax.random.uniform(key_rows, (REQS, SEGMENTS, TOK, 1), jnp.float32, 0.0, math.log(10.0)))
    normal_base = jax.random.truncated_normal(key_base, -4.0, 4.0, (REQS, SEGMENTS, TOK, D), jnp.float32)
    col_scale = jnp.exp(jax.random.uniform(key_cols, (D,), jnp.float32, 0.0, math.log(10.0)))
    return (normal_base * row_scale * col_scale).astype(jnp.bfloat16)


def draw_frames(key, part):
    key = jax.random.fold_in(key, 5)
    counts = jax.random.randint(key, (REQS, SEGMENTS), 1, FRAMES + 1)
    first = lax.iota(jnp.int32, SEGMENTS)[None, :] == 0
    return jnp.where(first, FRAMES, counts).astype(jnp.int32)


def set_ends(values, own_key, smallest, high):
    spot = [jax.random.randint(jax.random.fold_in(own_key, axis), (), 0, length) for axis, length in enumerate(values.shape)]
    longest = values.shape.index(max(values.shape))
    neighbour = spot[:longest] + [(spot[longest] + 1) % values.shape[longest]] + spot[longest + 1:]
    return values.at[tuple(spot)].set(smallest).at[tuple(neighbour)].set(high)


def block_scale(key, dims, shards, least, largest):
    def one(dim, parts):
        steps = jax.random.uniform(jax.random.fold_in(jax.random.fold_in(key, 6), dim), (parts,), jnp.float32, least / len(shards), largest / len(shards))
        return jnp.repeat(jnp.exp(steps), dims[dim] // parts).reshape((-1,) + (1,) * (len(dims) - dim - 1))

    loudness = one(*shards[0])
    for cut in shards[1:]:
        loudness = loudness * one(*cut)
    return loudness


def centred(rng, dims, deviation, reach, pieces=(), held_as=jnp.bfloat16):
    level = block_scale(rng, dims, pieces, -0.22, 0.18) if pieces else 1.0
    values = jax.random.normal(rng, dims, jnp.float32) * deviation * level
    return jnp.minimum(jnp.maximum(values, -reach), reach).astype(held_as)


def setup_inputs(seed: int = 0) -> dict:
    seeds = jax.random.split(jax.random.key(seed), 9)
    tokens = draw_tokens(jax.random.fold_in(seeds[8], 71), 0)
    levels = set_ends(jax.random.randint(seeds[1], (REQS, SEGMENTS), 0, LEVELS), jax.random.fold_in(seeds[1], 1), 0, LEVELS - 1).astype(jnp.int32)
    frames = draw_frames(jax.random.fold_in(seeds[8], 71), 0)
    segment_mask = set_ends((jax.random.randint(seeds[3], (REQS, SEGMENTS, SEGMENTS), 0, 4) < 3).astype(jnp.int32), jax.random.fold_in(seeds[3], 1), 0, 1)
    mod_table = centred(seeds[4], (LEVELS, 2, D), 0.5, 3.0, (), jnp.float32)
    w_qkv = centred(seeds[5], (D, H * 3 * HD), D ** -0.5, 0.109375, ((0, 4), (1, 8)))
    q_gain = jnp.clip(1.0 + 0.18 * jax.random.normal(seeds[6], (HD,), jnp.float32), 0.1, 1.9)
    k_gain = jnp.clip(1.0 + 0.18 * jax.random.normal(seeds[7], (HD,), jnp.float32), 0.1, 1.9)
    return {"tokens": tokens, "levels": levels, "frames": frames, "segment_mask": segment_mask, "mod_table": mod_table, "w_qkv": w_qkv, "q_gain": q_gain, "k_gain": k_gain}


EPS = 1e-06

def rms_scale(inputs):
    return lax.rsqrt(lax.optimization_barrier(jnp.mean(inputs * inputs, axis=-1, keepdims=True)) + EPS)

def reference(tokens, levels, frames, segment_mask, mod_table, w_qkv, q_gain, k_gain):
    mod_rows = mod_table[levels]
    widened = tokens.astype(jnp.float32)
    normed = (widened * rms_scale(widened) * (1.0 + mod_rows[:, :, 0, :][:, :, None, :]) + mod_rows[:, :, 1, :][:, :, None, :]).astype(jnp.bfloat16)
    score_scale = HD ** (-0.5)
    seq_span = SEGMENTS * TOK
    key_segment = jnp.arange(seq_span, dtype=jnp.int32) // TOK
    key_frame = jnp.arange(seq_span, dtype=jnp.int32) % TOK // TPF

    def one_request(items):
        token_rows, counts, mask_rows = items
        projected = jnp.dot(token_rows.reshape(seq_span, D), w_qkv, preferred_element_type=jnp.float32).reshape(seq_span, H, 3, HD)
        query_part = projected[:, :, 0]
        key_part = projected[:, :, 1]
        queries = (query_part * rms_scale(query_part) * q_gain).astype(jnp.bfloat16)
        key_heads = (key_part * rms_scale(key_part) * k_gain).astype(jnp.bfloat16)
        values = projected[:, :, 2].astype(jnp.bfloat16)
        queries, key_heads, values = lax.optimization_barrier((queries, key_heads, values))
        queries = queries.astype(jnp.float32)
        key_heads = key_heads.astype(jnp.float32)
        values = values.astype(jnp.float32)
        valid = key_frame < counts[key_segment]
        outputs_list = []
        for segment in range(SEGMENTS):
            earlier = mask_rows[segment][key_segment] == 1
            keep_mask = valid & ((key_segment == segment) | (key_segment < segment) & earlier)
            scores = jnp.einsum('qhe,khe->hqk', queries[segment * TOK:(segment + 1) * TOK], key_heads) * score_scale
            exp_scores = jnp.where(keep_mask[None, None, :], jnp.exp(scores), 0.0)
            denominator = lax.optimization_barrier(jnp.sum(exp_scores, axis=-1))
            weights = lax.optimization_barrier(exp_scores.astype(jnp.bfloat16)).astype(jnp.float32)
            numerator = jnp.einsum('hqk,khe->qhe', weights, values)
            result = (numerator / jnp.transpose(denominator)[:, :, None]).astype(jnp.bfloat16)
            outputs_list.append(result.reshape(TOK, H * HD))
        return jnp.stack(outputs_list)
    return lax.map(one_request, (normed, frames, segment_mask))
```

```python
import functools
import math

import jax
import jax.numpy as jnp
from jax import lax
from jax.experimental import pallas as pl
from jax.experimental.pallas import tpu as pltpu
from jax.sharding import PartitionSpec as P

HD = 128
TPF = 64
EPS = 1e-06
MIB = 1 << 20

HALVES, CORES, XS, YS = 2, 2, 4, 4
RING_Y = HALVES * YS


def place(y, core, x):
    return ((y // YS) * CORES + core) * (XS * YS) + x * YS + y % YS


def pairs(move, keep=lambda y: True):
    out = []
    for y in range(RING_Y):
        for core in range(CORES):
            for x in range(XS):
                if keep(y):
                    out.append((place(y, core, x), place(*move(y, core, x))))
    return out


MIRROR = pairs(lambda y, core, x: (RING_Y - 1 - y, core, x))
X_UP = pairs(lambda y, core, x: (y, core, (x + 1) % XS))
X_DOWN = pairs(lambda y, core, x: (y, core, (x - 1) % XS))
SWAP = pairs(lambda y, core, x: (y, 1 - core, x))
UP_FIRST = pairs(lambda y, core, x: (y + 2, core, x), lambda y: y < 4)
UP_SECOND = pairs(lambda y, core, x: (y + 2, core, x), lambda y: 2 <= y < 6)
DOWN_FIRST = pairs(lambda y, core, x: ((y - 2) % 8, core, x), lambda y: y < 4)
DOWN_SECOND = pairs(lambda y, core, x: (y - 2 if y >= 6 else y + 6, core, x), lambda y: y >= 6 or y < 2)


def move(array, table):
    return lax.ppermute(array, ("block", "req"), table)


def turn(array, step, size):
    return lax.ppermute(array, "head", [(i, (i + step) % size) for i in range(size)])


def project_kernel(n_pieces, spots_ref, *refs):
    spot = spots_ref
    (own, r1, l1, r2, l2, r3, l3, r4, l4, mod, gains, w_own, w_pair) = refs[:13]
    pieces = refs[13 : 13 + n_pieces]
    q_out, lo_out, hi_out = refs[13 + n_pieces : 16 + n_pieces]
    weight, normed, sems = refs[16 + n_pieces :]

    copies = []
    for number, source in enumerate((w_own, w_pair) + tuple(pieces)):
        rows = source.shape[0]
        start = pl.multiple_of(spot[8 + number], 96)
        copies.append(pltpu.make_async_copy(source, weight.at[pl.ds(start, rows), :], sems.at[number]))
    for copy in copies:
        copy.start()

    depth = own.shape[1]
    half = own.shape[0] // 2
    features = normed.shape[1]
    step_rows = 64

    for side, last in ((0, r4), (1, l4)):
        def norm_rows(step, carry, side=side, last=last):
            inner = pl.multiple_of(step * step_rows, step_rows)
            outer = pl.multiple_of(side * half + step * step_rows, step_rows)
            views = [ref.at[pl.ds(outer, step_rows), :] for ref in (own, r1, l1, r2, l2, r3, l3)]
            views.append(last.at[pl.ds(inner, step_rows), :])
            total = jnp.zeros((step_rows, 128), jnp.float32)
            for view in views:
                wide = view[...].astype(jnp.float32)
                square = wide * wide
                for lane in range(0, depth, 128):
                    total = total + square[:, lane : lane + 128]
            scale = lax.rsqrt(jnp.sum(total, axis=-1, keepdims=True) * (1.0 / features) + EPS)
            for number, view in enumerate(views):
                part = spot[number]
                wide = view[...].astype(jnp.float32)
                row = wide * scale * mod[0, part] + mod[1, part]
                column = pl.multiple_of(part * depth, 128)
                normed[pl.ds(outer, step_rows), pl.ds(column, depth)] = row.astype(jnp.bfloat16)
            return carry

        lax.fori_loop(0, half // step_rows, norm_rows, 0)

    for copy in copies:
        copy.wait()

    heads = q_out.shape[1] // HD

    def head_norm(part, gain):
        scale = lax.rsqrt(jnp.mean(part * part, axis=-1, keepdims=True) + EPS)
        return (part * scale * gain).astype(jnp.bfloat16)

    for head in range(heads):
        out = jnp.dot(
            normed[...], weight[:, 3 * HD * head : 3 * HD * (head + 1)], preferred_element_type=jnp.float32
        )
        q_out[:, HD * head : HD * (head + 1)] = head_norm(out[:, :HD], gains[0:1, :])
        keys = head_norm(out[:, HD : 2 * HD], gains[1:2, :])
        values = out[:, 2 * HD :].astype(jnp.bfloat16)
        at_k, at_v = HD * head, HD * (heads + head)
        lo_out[:, at_k : at_k + HD] = keys[:half]
        hi_out[:, at_k : at_k + HD] = keys[half:]
        lo_out[:, at_v : at_v + HD] = values[:half]
        hi_out[:, at_v : at_v + HD] = values[half:]


def attend_part(limit, first, q, kv, num, den, heads):
    rows = 256
    keys = kv.shape[0]
    column = lax.broadcasted_iota(jnp.int32, (1, keys), 1) + first
    keep = column < limit
    factor = HD ** (-0.5) * math.log2(math.e)
    for head in range(heads):
        span = slice(HD * head, HD * (head + 1))
        k = kv[:, span]
        v = kv[:, HD * (heads + head) : HD * (heads + head + 1)]
        for top in range(0, q.shape[0], rows):
            band = slice(top, top + rows)
            scores = lax.dot_general(
                q[band, span], k, (((1,), (1,)), ((), ())), preferred_element_type=jnp.float32
            )
            weights = jnp.where(keep, jnp.exp2(scores * factor), 0.0)
            total = weights[:, :128]
            for lane in range(128, keys, 128):
                total = total + weights[:, lane : lane + 128]
            den[band, span] += total
            num[band, span] += jnp.dot(weights.astype(jnp.bfloat16), v, preferred_element_type=jnp.float32)


def near_kernel(limits, q, lo, hi, pair_lo, pair_hi, num, den):
    heads = q.shape[1] // HD
    half = lo.shape[0]
    num[...] = jnp.zeros_like(num)
    den[...] = jnp.zeros_like(den)
    for slot, (low, high) in enumerate(((lo, hi), (pair_lo, pair_hi))):
        for first, part in ((0, low), (half, high)):
            @pl.when(limits[slot] > first)
            def _(slot=slot, first=first, part=part):
                attend_part(limits[slot], first, q, part, num, den, heads)


def far_kernel(limits, q, num_in, den_in, lo, hi, pair_lo, pair_hi, out, num, den):
    heads = q.shape[1] // HD
    half = lo.shape[0]
    num[...] = num_in[...]
    den[...] = den_in[...]
    for slot, (low, high) in enumerate(((lo, hi), (pair_lo, pair_hi))):
        for first, part in ((0, low), (half, high)):
            @pl.when(limits[2 + slot] > first)
            def _(slot=slot, first=first, part=part):
                attend_part(limits[2 + slot], first, q, part, num, den, heads)
    for head in range(heads):
        span = slice(HD * head, HD * (head + 1))
        total = jnp.sum(den[:, span], axis=-1, keepdims=True)
        out[:, span] = (num[:, span] / total).astype(jnp.bfloat16)


def body(tokens, levels, frames, segment_mask, mod_table, w_qkv, q_gain, k_gain):
    own = tokens[0, 0]
    rows, depth = own.shape
    ring = mod_table.shape[2] // depth
    columns = w_qkv.shape[1]
    heads = columns // (3 * HD)
    part_rows = w_qkv.shape[0]
    quarter = part_rows // XS
    piece = quarter // 2

    z = lax.axis_index("head")
    block = lax.axis_index("block")
    side, core = block // CORES, block % CORES
    x = lax.axis_index("req") // YS

    ya = move(lax.dynamic_slice_in_dim(w_qkv, quarter * x, piece), MIRROR)
    r1, l1 = turn(own, 1, ring), turn(own, -1, ring)
    yb = move(lax.dynamic_slice_in_dim(w_qkv, quarter * x + piece, piece), MIRROR)
    w_pair = move(w_qkv, SWAP)
    r2, l2 = turn(r1, 1, ring), turn(l1, -1, ring)
    a_up, a_down = move(ya, X_UP), move(ya, X_DOWN)
    b_up, b_down = move(yb, X_UP), move(yb, X_DOWN)
    r3, l3 = turn(r2, 1, ring), turn(l2, -1, ring)
    a_far = move(a_up, X_UP)
    b_far = move(b_down, X_DOWN)
    r4, l4 = turn(r3[: rows // 2], 1, ring), turn(l3[rows // 2 :], -1, ring)
    up, down, far = (x + XS - 1) % XS, (x + 1) % XS, (x + 2) % XS
    held = [(ya, x, 0), (yb, x, 1), (a_up, up, 0), (a_down, down, 0), (b_up, up, 1), (b_down, down, 1),
            (a_far, far, 0), (b_far, far, 1)]
    other_side = 1 - side
    arrays, starts = [], []
    for array, which, sub in held:
        at = which * quarter + sub * piece
        arrays += [array, move(array, SWAP)]
        starts += [(other_side * CORES + core) * part_rows + at, (other_side * CORES + 1 - core) * part_rows + at]

    order = [z, z - 1, z + 1, z - 2, z + 2, z - 3, z + 3, z + 4]
    spots = [(item + ring) % ring for item in order]
    spots += [block * part_rows, (side * CORES + 1 - core) * part_rows] + starts
    spots = jnp.stack(spots).astype(jnp.int32)

    mod_rows = lax.dynamic_index_in_dim(mod_table, levels[0, 0], 0, keepdims=False)
    mod = (mod_rows + jnp.array([[1.0], [0.0]], jnp.float32)).reshape(2, ring, 1, depth)
    gains = jnp.stack([q_gain, k_gain])

    smem = pl.BlockSpec(memory_space=pltpu.SMEM)
    vmem = pl.BlockSpec(memory_space=pltpu.VMEM)
    anywhere = pl.BlockSpec(memory_space=pl.ANY)
    n = len(arrays)
    queries, kv_lo, kv_hi = pl.pallas_call(
        functools.partial(project_kernel, n),
        out_shape=(
            jax.ShapeDtypeStruct((rows, heads * HD), jnp.bfloat16),
            jax.ShapeDtypeStruct((rows // 2, 2 * heads * HD), jnp.bfloat16),
            jax.ShapeDtypeStruct((rows // 2, 2 * heads * HD), jnp.bfloat16),
        ),
        in_specs=[smem] + [vmem] * 11 + [anywhere] * (2 + n),
        out_specs=(vmem, vmem, vmem),
        scratch_shapes=[
            pltpu.VMEM((ring * depth, columns), jnp.bfloat16),
            pltpu.VMEM((rows, ring * depth), jnp.bfloat16),
            pltpu.SemaphoreType.DMA((2 + n,)),
        ],
        compiler_params=pltpu.CompilerParams(vmem_limit_bytes=32 * MIB),
        cost_estimate=pl.CostEstimate(
            flops=2 * rows * ring * depth * columns, bytes_accessed=12 * MIB, transcendentals=0
        ),
        name="project",
    )(spots, own, r1, l1, r2, l2, r3, l3, r4, l4, mod, gains, w_qkv, w_pair, *arrays)

    far_lo = move(kv_lo, UP_FIRST)
    far_hi = move(kv_hi, DOWN_FIRST)
    pair_lo, pair_hi = move(kv_lo, SWAP), move(kv_hi, SWAP)
    far_lo = move(far_lo, UP_SECOND)
    far_hi = move(far_hi, DOWN_SECOND)
    far_pair_lo, far_pair_hi = move(far_lo, SWAP), move(far_hi, SWAP)

    def limit(segment):
        seen = (segment == block) | (segment < block) & (segment_mask[0, block, segment] == 1)
        return jnp.where(seen, frames[0, segment] * TPF, 0)

    pair = side * CORES + 1 - core
    limits = [limit(item) for item in (block, pair, other_side * CORES + core, other_side * CORES + 1 - core)]
    limits = jnp.stack(limits).astype(jnp.int32)

    sums = jax.ShapeDtypeStruct((rows, heads * HD), jnp.float32)
    work = pl.CostEstimate(
        flops=8 * rows * rows * heads * HD, bytes_accessed=6 * MIB, transcendentals=2 * rows * rows * heads
    )
    num, den = pl.pallas_call(
        near_kernel,
        out_shape=(sums, sums),
        in_specs=[smem] + [vmem] * 5,
        out_specs=(vmem, vmem),
        compiler_params=pltpu.CompilerParams(vmem_limit_bytes=32 * MIB),
        cost_estimate=work,
        name="near",
    )(limits, queries, kv_lo, kv_hi, pair_lo, pair_hi)
    result = pl.pallas_call(
        far_kernel,
        out_shape=jax.ShapeDtypeStruct((rows, heads * HD), jnp.bfloat16),
        in_specs=[smem] + [vmem] * 7,
        out_specs=vmem,
        scratch_shapes=[pltpu.VMEM((rows, heads * HD), jnp.float32)] * 2,
        compiler_params=pltpu.CompilerParams(vmem_limit_bytes=32 * MIB),
        cost_estimate=work,
        name="far",
    )(limits, queries, num, den, far_lo, far_hi, far_pair_lo, far_pair_hi)
    return result.reshape(1, 1, rows, heads * HD)


def solution(mesh):
    placed = (
        P("req", "block", None, "head"),
        P("req", "block"),
        P("req", None),
        P("req", None, None),
        P(),
        P("block", "head"),
        P(),
        P(),
    )
    return jax.shard_map(
        body, mesh=mesh, in_specs=placed, out_specs=P("req", "block", None, "head"), check_vma=False
    )
```

```python
import math

import jax
import jax.numpy as jnp
from jax import lax
from jax.experimental import pallas as pl
from jax.experimental.pallas import tpu as pltpu
from jax.sharding import PartitionSpec as P

HD = 128
TPF = 64
EPS = 1e-06
MIB = 1 << 20

HALVES, CORES, XS, YS = 2, 2, 4, 4
RING_Y = HALVES * YS


def place(y, core, x):
    return ((y // YS) * CORES + core) * (XS * YS) + x * YS + y % YS


def pairs(move, keep=lambda y: True):
    out = []
    for y in range(RING_Y):
        for core in range(CORES):
            for x in range(XS):
                if keep(y):
                    out.append((place(y, core, x), place(*move(y, core, x))))
    return out


MIRROR = pairs(lambda y, core, x: (RING_Y - 1 - y, core, x))
X_RING = pairs(lambda y, core, x: (y, core, (x + 1 - 2 * core) % XS))
SWAP = pairs(lambda y, core, x: (y, 1 - core, x))
UP_FIRST = pairs(lambda y, core, x: (y + 2, core, x), lambda y: y < 4)
UP_SECOND = pairs(lambda y, core, x: (y + 2, core, x), lambda y: 2 <= y < 6)
DOWN_FIRST = pairs(lambda y, core, x: ((y - 2) % 8, core, x), lambda y: y < 4)
DOWN_SECOND = pairs(lambda y, core, x: (y - 2 if y >= 6 else y + 6, core, x), lambda y: y >= 6 or y < 2)


def move(array, table):
    return lax.ppermute(array, ("block", "req"), table)


def turn(array, step, size):
    return lax.ppermute(array, "head", [(i, (i + step) % size) for i in range(size)])


def gather_kernel(spots, levels, *refs):
    (own, r1, l1, r2, l2, r3, l3, r4, l4, mod, w_own, w_pair, w_rest) = refs[:13]
    acc, last_columns, normed = refs[13:]
    rows, depth = own.shape
    half = rows // 2
    features = normed.shape[1]
    step_rows = 64
    level = levels[0, 0]

    for side, last in ((0, r4), (1, l4)):
        def norm_rows(step, carry, side=side, last=last):
            inner = pl.multiple_of(step * step_rows, step_rows)
            outer = pl.multiple_of(side * half + step * step_rows, step_rows)
            views = [ref.at[pl.ds(outer, step_rows), :] for ref in (own, r1, l1, r2, l2, r3, l3)]
            views.append(last.at[pl.ds(inner, step_rows), :])
            total = jnp.zeros((step_rows, 128), jnp.float32)
            for view in views:
                wide = view[...].astype(jnp.float32)
                square = wide * wide
                for lane in range(0, depth, 128):
                    total = total + square[:, lane : lane + 128]
            scale = lax.rsqrt(jnp.sum(total, axis=-1, keepdims=True) * (1.0 / features) + EPS)
            for number, view in enumerate(views):
                column = pl.multiple_of(spots[number] * depth, 128)
                wide = view[...].astype(jnp.float32)
                gain = 1.0 + mod[level, 0:1, pl.ds(column, depth)]
                row = wide * scale * gain + mod[level, 1:2, pl.ds(column, depth)]
                normed[pl.ds(outer, step_rows), pl.ds(column, depth)] = row.astype(jnp.bfloat16)
            return carry

        lax.fori_loop(0, half // step_rows, norm_rows, 0)

    part = w_own.shape[0]
    columns = acc.shape[1]

    def block_of(number):
        return normed[:, pl.ds(pl.multiple_of(spots[8 + number] * part, 128), part)]

    for start in range(0, columns, 512):
        span = slice(start, min(start + 512, columns))
        total = jnp.dot(block_of(0), w_own[:, span], preferred_element_type=jnp.float32)
        total += jnp.dot(block_of(1), w_pair[:, span], preferred_element_type=jnp.float32)
        total += jnp.dot(block_of(2), w_rest[:, span], preferred_element_type=jnp.float32)
        acc[:, span] = total
    last_columns[...] = block_of(3)


def project_kernel(acc, last_columns, w_last, q_gain, k_gain, q_out, kv_out):
    heads = q_out.shape[1] // HD

    def head_norm(part, gain):
        scale = lax.rsqrt(jnp.mean(part * part, axis=-1, keepdims=True) + EPS)
        return (part * scale * gain).astype(jnp.bfloat16)

    for head in range(heads):
        span = slice(3 * HD * head, 3 * HD * (head + 1))
        out = acc[:, span] + jnp.dot(last_columns[...], w_last[:, span], preferred_element_type=jnp.float32)
        q_out[:, HD * head : HD * (head + 1)] = head_norm(out[:, :HD], q_gain[...])
        kv_out[:, HD * head : HD * (head + 1)] = head_norm(out[:, HD : 2 * HD], k_gain[...])
        kv_out[:, HD * (heads + head) : HD * (heads + head + 1)] = out[:, 2 * HD :].astype(jnp.bfloat16)


def key_limit(spots, frames, mask, number):
    block, segment = spots[8], spots[8 + number]
    seen = (segment == block) | ((segment < block) & (mask[block, segment] == 1))
    return jnp.where(seen, frames[0, segment] * TPF, 0)


def attend_part(limit, first, q, kv, num, den, heads):
    rows = 256
    keys = kv.shape[0]
    column = lax.broadcasted_iota(jnp.int32, (1, keys), 1) + first
    keep = column < limit
    factor = HD ** (-0.5) * math.log2(math.e)
    for head in range(heads):
        span = slice(HD * head, HD * (head + 1))
        k = kv[:, span]
        v = kv[:, HD * (heads + head) : HD * (heads + head + 1)]
        for top in range(0, q.shape[0], rows):
            band = slice(top, top + rows)
            scores = lax.dot_general(
                q[band, span], k, (((1,), (1,)), ((), ())), preferred_element_type=jnp.float32
            )
            weights = jnp.where(keep, jnp.exp2(scores * factor), 0.0)
            total = weights[:, :128]
            for lane in range(128, keys, 128):
                total = total + weights[:, lane : lane + 128]
            den[band, span] += total
            num[band, span] += jnp.dot(weights.astype(jnp.bfloat16), v, preferred_element_type=jnp.float32)


def near_kernel(spots, frames, mask, q, own, pair, num, den):
    heads = q.shape[1] // HD
    half = q.shape[0] // 2
    num[...] = jnp.zeros_like(num)
    den[...] = jnp.zeros_like(den)
    for number, kv in ((0, own), (1, pair)):
        limit = key_limit(spots, frames, mask, number)
        for first in (0, half):
            @pl.when(limit > first)
            def _(limit=limit, first=first, kv=kv):
                attend_part(limit, first, q, kv.at[first : first + half], num, den, heads)


def far_kernel(number, finish, spots, frames, mask, q, num_in, den_in, lo, hi, *rest):
    heads = q.shape[1] // HD
    half = q.shape[0] // 2
    num, den = rest[-2:]
    num[...] = num_in[...]
    den[...] = den_in[...]
    limit = key_limit(spots, frames, mask, number)
    for first, kv in ((0, lo), (half, hi)):
        @pl.when(limit > first)
        def _(first=first, kv=kv):
            attend_part(limit, first, q, kv, num, den, heads)
    if finish:
        for head in range(heads):
            span = slice(HD * head, HD * (head + 1))
            total = jnp.sum(den[:, span], axis=-1, keepdims=True)
            rest[0][:, span] = (num[:, span] / total).astype(jnp.bfloat16)


def body(tokens, levels, frames, segment_mask, mod_table, w_qkv, q_gain, k_gain):
    own = tokens[0, 0]
    rows, depth = own.shape
    ring = mod_table.shape[2] // depth
    part_rows, columns = w_qkv.shape
    heads = columns // (3 * HD)
    width = heads * HD
    quarter = part_rows // XS
    half = rows // 2

    z = lax.axis_index("head")
    block = lax.axis_index("block")
    side, core = block // CORES, block % CORES
    x = lax.axis_index("req") // YS

    piece = move(lax.dynamic_slice_in_dim(w_qkv, quarter * x, quarter), MIRROR)
    r1, l1 = turn(own, 1, ring), turn(own, -1, ring)
    w_pair = move(w_qkv, SWAP)
    r1, l1, w_pair = lax.optimization_barrier((r1, l1, w_pair))
    r2, l2 = turn(r1, 1, ring), turn(l1, -1, ring)
    piece, r2, l2 = lax.optimization_barrier((piece, r2, l2))
    held = [piece, move(piece, X_RING)]
    r3, l3 = turn(r2, 1, ring), turn(l2, -1, ring)
    held[1], r3, l3 = lax.optimization_barrier((held[1], r3, l3))
    held.append(move(held[1], X_RING))
    r4, l4 = turn(r3[:half], 1, ring), turn(l3[half:], -1, ring)
    held.append(move(held[2], X_RING))
    w_rest = jnp.zeros_like(w_qkv)
    for step, piece in enumerate(held):
        at = (x + (2 * core - 1) * step + XS) % XS
        w_rest = lax.dynamic_update_slice_in_dim(w_rest, piece, at * quarter, 0)
    w_rest, r4, l4 = lax.optimization_barrier((w_rest, r4, l4))
    w_last = move(w_rest, SWAP)

    order = [z, z - 1, z + 1, z - 2, z + 2, z - 3, z + 3, z + 4]
    spots = [(item + ring) % ring for item in order]
    other = (1 - side) * CORES
    spots += [block, side * CORES + 1 - core, other + core, other + 1 - core]
    spots = jnp.stack(spots).astype(jnp.int32)

    smem = pl.BlockSpec(memory_space=pltpu.SMEM)
    vmem = pl.BlockSpec(memory_space=pltpu.VMEM)

    def sized(limit):
        return pltpu.CompilerParams(vmem_limit_bytes=limit * MIB)

    acc, last_columns = pl.pallas_call(
        gather_kernel,
        out_shape=(
            jax.ShapeDtypeStruct((rows, columns), jnp.float32),
            jax.ShapeDtypeStruct((rows, part_rows), jnp.bfloat16),
        ),
        in_specs=[smem] * 2 + [vmem] * 13,
        out_specs=(vmem, vmem),
        scratch_shapes=[pltpu.VMEM((rows, ring * depth), jnp.bfloat16)],
        compiler_params=sized(32),
        cost_estimate=pl.CostEstimate(
            flops=2 * rows * 3 * part_rows * columns, bytes_accessed=12 * MIB, transcendentals=0
        ),
        name="gather",
    )(spots, levels, own, r1, l1, r2, l2, r3, l3, r4, l4, mod_table, w_qkv, w_pair, w_rest)
    queries, kv = pl.pallas_call(
        project_kernel,
        out_shape=(
            jax.ShapeDtypeStruct((rows, width), jnp.bfloat16),
            jax.ShapeDtypeStruct((rows, 2 * width), jnp.bfloat16),
        ),
        in_specs=[vmem] * 5,
        out_specs=(vmem, vmem),
        compiler_params=sized(24),
        cost_estimate=pl.CostEstimate(
            flops=2 * rows * part_rows * columns, bytes_accessed=6 * MIB, transcendentals=0
        ),
        name="project",
    )(acc, last_columns, w_last, q_gain[None, :], k_gain[None, :])

    far_lo = move(kv[:half], UP_FIRST)
    far_hi = move(kv[half:], DOWN_FIRST)
    pair_kv = move(kv, SWAP)

    where = (spots, frames, segment_mask[0])
    sums = (jax.ShapeDtypeStruct((rows, width), jnp.float32),) * 2
    work = pl.CostEstimate(
        flops=8 * rows * rows * width, bytes_accessed=6 * MIB, transcendentals=2 * rows * rows * heads
    )
    num, den = pl.pallas_call(
        near_kernel,
        out_shape=sums,
        in_specs=[smem] * 3 + [vmem] * 3,
        out_specs=(vmem, vmem),
        compiler_params=sized(24),
        cost_estimate=work,
        name="near",
    )(*where, queries, kv, pair_kv)
    far_lo, far_hi, num, den = lax.optimization_barrier((far_lo, far_hi, num, den))
    far_lo = move(far_lo, UP_SECOND)
    far_hi = move(far_hi, DOWN_SECOND)
    far_kv = lax.optimization_barrier(jnp.concatenate([far_lo, far_hi]))
    far_pair = move(far_kv, SWAP)
    num, den = pl.pallas_call(
        lambda *refs: far_kernel(2, False, *refs),
        out_shape=sums,
        in_specs=[smem] * 3 + [vmem] * 5,
        out_specs=(vmem, vmem),
        compiler_params=sized(24),
        cost_estimate=work,
        name="far",
    )(*where, queries, num, den, far_lo, far_hi)
    result = pl.pallas_call(
        lambda *refs: far_kernel(3, True, *refs),
        out_shape=jax.ShapeDtypeStruct((rows, width), jnp.bfloat16),
        in_specs=[smem] * 3 + [vmem] * 5,
        out_specs=vmem,
        scratch_shapes=[pltpu.VMEM((rows, width), jnp.float32)] * 2,
        compiler_params=sized(24),
        cost_estimate=work,
        name="last",
    )(*where, queries, num, den, far_pair[:half], far_pair[half:])
    return result.reshape(1, 1, rows, width)


def solution(mesh):
    placed = (
        P("req", "block", None, "head"),
        P("req", "block"),
        P("req", None),
        P("req", None, None),
        P(),
        P("block", "head"),
        P(),
        P(),
    )
    return jax.shard_map(
        body, mesh=mesh, in_specs=placed, out_specs=P("req", "block", None, "head"), check_vma=False
    )
```

```python
import math

import jax
import jax.numpy as jnp
from jax import lax
from jax.experimental import pallas as pl
from jax.experimental.pallas import tpu as pltpu
from jax.sharding import PartitionSpec as P

HD = 128
TPF = 64
EPS = 1e-06
MIB = 1 << 20

HALVES, CORES, XS, YS = 2, 2, 4, 4
RING_Y = HALVES * YS


def place(y, core, x):
    return ((y // YS) * CORES + core) * (XS * YS) + x * YS + y % YS


def pairs(move, keep=lambda y: True):
    out = []
    for y in range(RING_Y):
        for core in range(CORES):
            for x in range(XS):
                if keep(y):
                    out.append((place(y, core, x), place(*move(y, core, x))))
    return out


MIRROR = pairs(lambda y, core, x: (RING_Y - 1 - y, core, x))
X_RING = pairs(lambda y, core, x: (y, core, (x + 1 - 2 * core) % XS))
SWAP = pairs(lambda y, core, x: (y, 1 - core, x))
FIRST = pairs(lambda y, core, x: ((y + 2 - 4 * core) % RING_Y, core, x), lambda y: y < YS)
SECOND = [(b, place((y + 4) % RING_Y, core, x)) for y in range(YS) for core in range(CORES) for x in range(XS)
          for b in [place((y + 2 - 4 * core) % RING_Y, core, x)]]


def move(array, table):
    return lax.ppermute(array, ("block", "req"), table)


def turn(array, size):
    per_block = XS * YS * size
    table = []
    for block in range(HALVES * CORES):
        step = 1 - 2 * (block % CORES)
        for other in range(XS * YS):
            base = block * per_block + other * size
            table += [(base + i, base + (i + step) % size) for i in range(size)]
    return lax.ppermute(array, ("block", "req", "head"), table)


def gather_kernel(spots, levels, *refs):
    pieces = refs[:8]
    mod_table, w_own_far, w_pair_far, w_rest = refs[8:12]
    acc, last_columns, tokens, mod, w_own, w_pair, normed, sems = refs[12:]
    rows, depth = pieces[0].shape
    features = normed.shape[1]
    step_rows = 64

    loads = [pltpu.make_async_copy(piece, tokens.at[number], sems.at[number]) for number, piece in enumerate(pieces)]
    loads.append(pltpu.make_async_copy(mod_table.at[levels[0, 0]], mod, sems.at[8]))
    weights = [
        pltpu.make_async_copy(w_own_far, w_own, sems.at[9]),
        pltpu.make_async_copy(w_pair_far, w_pair, sems.at[10]),
    ]
    for copy in loads + weights:
        copy.start()
    for copy in loads:
        copy.wait()

    def norm_rows(step, carry):
        band = pl.ds(pl.multiple_of(step * step_rows, step_rows), step_rows)
        total = jnp.zeros((step_rows, 128), jnp.float32)
        for number in range(8):
            wide = tokens[number, band, :].astype(jnp.float32)
            square = wide * wide
            for lane in range(0, depth, 128):
                total = total + square[:, lane : lane + 128]
        scale = lax.rsqrt(jnp.sum(total, axis=-1, keepdims=True) * (1.0 / features) + EPS)
        for number in range(8):
            column = pl.multiple_of(spots[number] * depth, 128)
            wide = tokens[number, band, :].astype(jnp.float32)
            row = wide * scale * (1.0 + mod[0:1, pl.ds(column, depth)]) + mod[1:2, pl.ds(column, depth)]
            normed[band, pl.ds(column, depth)] = row.astype(jnp.bfloat16)
        return carry

    lax.fori_loop(0, rows // step_rows, norm_rows, 0)
    for copy in weights:
        copy.wait()

    part = w_own.shape[0]
    columns = acc.shape[1]

    def block_of(number):
        return normed[:, pl.ds(pl.multiple_of(spots[8 + number] * part, 128), part)]

    for start in range(0, columns, 512):
        span = slice(start, min(start + 512, columns))
        total = jnp.dot(block_of(0), w_own[:, span], preferred_element_type=jnp.float32)
        total += jnp.dot(block_of(1), w_pair[:, span], preferred_element_type=jnp.float32)
        total += jnp.dot(block_of(2), w_rest[:, span], preferred_element_type=jnp.float32)
        acc[:, span] = total
    last_columns[...] = block_of(3)


def project_kernel(acc, last_columns, w_last, q_gain, k_gain, q_out, kv_out):
    heads = q_out.shape[1] // HD

    def head_norm(part, gain):
        scale = lax.rsqrt(jnp.mean(part * part, axis=-1, keepdims=True) + EPS)
        return (part * scale * gain).astype(jnp.bfloat16)

    for head in range(heads):
        span = slice(3 * HD * head, 3 * HD * (head + 1))
        out = acc[:, span] + jnp.dot(last_columns[...], w_last[:, span], preferred_element_type=jnp.float32)
        q_out[:, HD * head : HD * (head + 1)] = head_norm(out[:, :HD], q_gain[...])
        kv_out[:, HD * head : HD * (head + 1)] = head_norm(out[:, HD : 2 * HD], k_gain[...])
        kv_out[:, HD * (heads + head) : HD * (heads + head + 1)] = out[:, 2 * HD :].astype(jnp.bfloat16)


def key_limit(spots, frames, mask, number):
    block, segment = spots[8], spots[8 + number]
    seen = (segment == block) | ((segment < block) & (mask[block, segment] == 1))
    return jnp.where(seen, frames[0, segment] * TPF, 0)


def attend_part(limit, first, q, kv, num, den, heads):
    rows = 256
    keys = kv.shape[0]
    column = lax.broadcasted_iota(jnp.int32, (1, keys), 1) + first
    keep = column < limit
    factor = HD ** (-0.5) * math.log2(math.e)
    for head in range(heads):
        span = slice(HD * head, HD * (head + 1))
        k = kv[:, span]
        v = kv[:, HD * (heads + head) : HD * (heads + head + 1)]
        for top in range(0, q.shape[0], rows):
            band = slice(top, top + rows)
            scores = lax.dot_general(
                q[band, span], k, (((1,), (1,)), ((), ())), preferred_element_type=jnp.float32
            )
            weights = jnp.where(keep, jnp.exp2(scores * factor), 0.0)
            total = weights[:, :128]
            for lane in range(128, keys, 128):
                total = total + weights[:, lane : lane + 128]
            den[band, span] += total
            num[band, span] += jnp.dot(weights.astype(jnp.bfloat16), v, preferred_element_type=jnp.float32)


def near_kernel(spots, frames, mask, q, own, pair, num, den):
    heads = q.shape[1] // HD
    half = q.shape[0] // 2
    num[...] = jnp.zeros_like(num)
    den[...] = jnp.zeros_like(den)
    for number, kv in ((0, own), (1, pair)):
        limit = key_limit(spots, frames, mask, number)
        for first in (0, half):
            @pl.when(limit > first)
            def _(limit=limit, first=first, kv=kv):
                attend_part(limit, first, q, kv.at[first : first + half], num, den, heads)


def far_kernel(number, finish, spots, frames, mask, q, num_in, den_in, kv, *rest):
    heads = q.shape[1] // HD
    half = q.shape[0] // 2
    num, den = rest[-2:]
    num[...] = num_in[...]
    den[...] = den_in[...]
    limit = key_limit(spots, frames, mask, number)
    for first in (0, half):
        @pl.when(limit > first)
        def _(first=first):
            attend_part(limit, first, q, kv.at[first : first + half], num, den, heads)
    if finish:
        for head in range(heads):
            span = slice(HD * head, HD * (head + 1))
            total = jnp.sum(den[:, span], axis=-1, keepdims=True)
            rest[0][:, span] = (num[:, span] / total).astype(jnp.bfloat16)


def body(tokens, levels, frames, segment_mask, mod_table, w_qkv, q_gain, k_gain):
    own = tokens[0, 0]
    rows, depth = own.shape
    ring = mod_table.shape[2] // depth
    part_rows, columns = w_qkv.shape
    heads = columns // (3 * HD)
    width = heads * HD
    quarter = part_rows // XS

    z = lax.axis_index("head")
    block = lax.axis_index("block")
    side, core = block // CORES, block % CORES
    x = lax.axis_index("req") // YS

    mine = [lax.dynamic_slice_in_dim(w_qkv, quarter * x + at, quarter // 2) for at in (0, quarter // 2)]
    first, second = (move(item, MIRROR) for item in mine)
    w_pair = move(w_qkv, SWAP)
    pieces = [own, turn(own, ring)]
    pieces.append(turn(pieces[1], ring))
    first, pieces[2] = lax.optimization_barrier((first, pieces[2]))
    pieces.append(turn(pieces[2], ring))
    first, second, w_pair, pieces[3] = lax.optimization_barrier((first, second, w_pair, pieces[3]))
    held = [jnp.concatenate([first, second])]
    for _ in range(XS - 1):
        following = turn(pieces[-1], ring)
        held.append(move(held[-1], X_RING))
        held[-1], following = lax.optimization_barrier((held[-1], following))
        pieces.append(following)
    pieces.append(turn(pieces[-1], ring))
    w_rest = jnp.zeros_like(w_qkv)
    for step, piece in enumerate(held):
        at = (x + (2 * core - 1) * step + XS) % XS
        w_rest = lax.dynamic_update_slice_in_dim(w_rest, piece, at * quarter, 0)
    w_last = move(w_rest, SWAP)

    spots = [(z + (2 * core - 1) * step + ring) % ring for step in range(ring)]
    other = (1 - side) * CORES
    spots += [block, side * CORES + 1 - core, other + core, other + 1 - core]
    spots = jnp.stack(spots).astype(jnp.int32)

    smem = pl.BlockSpec(memory_space=pltpu.SMEM)
    vmem = pl.BlockSpec(memory_space=pltpu.VMEM)
    anywhere = pl.BlockSpec(memory_space=pl.ANY)

    def sized(limit):
        return pltpu.CompilerParams(vmem_limit_bytes=limit * MIB)

    acc, last_columns = pl.pallas_call(
        gather_kernel,
        out_shape=(
            jax.ShapeDtypeStruct((rows, columns), jnp.float32),
            jax.ShapeDtypeStruct((rows, part_rows), jnp.bfloat16),
        ),
        in_specs=[smem] * 2 + [anywhere] * 11 + [vmem],
        out_specs=(vmem, vmem),
        scratch_shapes=[
            pltpu.VMEM((ring, rows, depth), jnp.bfloat16),
            pltpu.VMEM(mod_table.shape[1:], jnp.float32),
            pltpu.VMEM((part_rows, columns), jnp.bfloat16),
            pltpu.VMEM((part_rows, columns), jnp.bfloat16),
            pltpu.VMEM((rows, ring * depth), jnp.bfloat16),
            pltpu.SemaphoreType.DMA((11,)),
        ],
        compiler_params=sized(32),
        cost_estimate=pl.CostEstimate(
            flops=2 * rows * 3 * part_rows * columns, bytes_accessed=12 * MIB, transcendentals=0
        ),
        name="gather",
    )(spots, levels, *pieces, mod_table, w_qkv, w_pair, w_rest)
    queries, kv = pl.pallas_call(
        project_kernel,
        out_shape=(
            jax.ShapeDtypeStruct((rows, width), jnp.bfloat16),
            jax.ShapeDtypeStruct((rows, 2 * width), jnp.bfloat16),
        ),
        in_specs=[vmem] * 5,
        out_specs=(vmem, vmem),
        compiler_params=sized(24),
        cost_estimate=pl.CostEstimate(
            flops=2 * rows * part_rows * columns, bytes_accessed=6 * MIB, transcendentals=0
        ),
        name="project",
    )(acc, last_columns, w_last, q_gain[None, :], k_gain[None, :])

    far_kv = move(kv, FIRST)
    pair_kv = move(kv, SWAP)

    where = (spots, frames, segment_mask[0])
    sums = (jax.ShapeDtypeStruct((rows, width), jnp.float32),) * 2
    work = pl.CostEstimate(
        flops=8 * rows * rows * width, bytes_accessed=6 * MIB, transcendentals=2 * rows * rows * heads
    )
    num, den = pl.pallas_call(
        near_kernel,
        out_shape=sums,
        in_specs=[smem] * 3 + [vmem] * 3,
        out_specs=(vmem, vmem),
        compiler_params=sized(24),
        cost_estimate=work,
        name="near",
    )(*where, queries, kv, pair_kv)
    far_kv, num, den = lax.optimization_barrier((far_kv, num, den))
    far_kv = move(far_kv, SECOND)
    far_pair = move(far_kv, SWAP)
    num, den = pl.pallas_call(
        lambda *refs: far_kernel(2, False, *refs),
        out_shape=sums,
        in_specs=[smem] * 3 + [vmem] * 4,
        out_specs=(vmem, vmem),
        compiler_params=sized(24),
        cost_estimate=work,
        name="far",
    )(*where, queries, num, den, far_kv)
    result = pl.pallas_call(
        lambda *refs: far_kernel(3, True, *refs),
        out_shape=jax.ShapeDtypeStruct((rows, width), jnp.bfloat16),
        in_specs=[smem] * 3 + [vmem] * 4,
        out_specs=vmem,
        scratch_shapes=[pltpu.VMEM((rows, width), jnp.float32)] * 2,
        compiler_params=sized(24),
        cost_estimate=work,
        name="last",
    )(*where, queries, num, den, far_pair)
    return result.reshape(1, 1, rows, width)


def solution(mesh):
    placed = (
        P("req", "block", None, "head"),
        P("req", "block"),
        P("req", None),
        P("req", None, None),
        P(),
        P("block", "head"),
        P(),
        P(),
    )
    return jax.shard_map(
        body, mesh=mesh, in_specs=placed, out_specs=P("req", "block", None, "head"), check_vma=False
    )
```

```python
import functools
import math

import jax
import jax.numpy as jnp
from jax import lax
from jax.experimental import pallas as pl
from jax.experimental.pallas import tpu as pltpu
from jax.sharding import PartitionSpec as P

HD = 128
TPF = 64
EPS = 1e-06
MIB = 1 << 20

HALVES, CORES, XS, YS = 2, 2, 4, 4
RING_Y = HALVES * YS


def place(y, core, x):
    return ((y // YS) * CORES + core) * (XS * YS) + x * YS + y % YS


def pairs(move, keep=lambda y: True):
    out = []
    for y in range(RING_Y):
        for core in range(CORES):
            for x in range(XS):
                if keep(y):
                    out.append((place(y, core, x), place(*move(y, core, x))))
    return out


MIRROR = pairs(lambda y, core, x: (RING_Y - 1 - y, core, x))
X_UP = pairs(lambda y, core, x: (y, core, (x + 1) % XS))
X_DOWN = pairs(lambda y, core, x: (y, core, (x - 1) % XS))
SWAP = pairs(lambda y, core, x: (y, 1 - core, x))
UP_FIRST = pairs(lambda y, core, x: (y + 2, core, x), lambda y: y < 4)
UP_SECOND = pairs(lambda y, core, x: (y + 2, core, x), lambda y: 2 <= y < 6)
DOWN_FIRST = pairs(lambda y, core, x: ((y - 2) % 8, core, x), lambda y: y < 4)
DOWN_SECOND = pairs(lambda y, core, x: (y - 2 if y >= 6 else y + 6, core, x), lambda y: y >= 6 or y < 2)


def move(array, table):
    return lax.ppermute(array, ("block", "req"), table)


def project_kernel(n_pieces, starts, levels, *refs):
    tokens_far, table, q_gain, k_gain = refs[:4]
    pieces = refs[4 : 4 + n_pieces]
    q_out, kv_out, lo_out, hi_out, tokens, mod, weight, normed, token_sems, mod_sem, sems = refs[4 + n_pieces :]
    parts, rows, depth = tokens.shape
    features = parts * depth
    chunks = token_sems.shape[0]
    chunk = rows // chunks
    step_rows = 64

    mod_load = pltpu.make_async_copy(table.at[levels[0, 0]], mod, mod_sem)
    mod_load.start()
    loads = []
    for number in range(chunks):
        band = pl.ds(number * chunk, chunk)
        loads.append(pltpu.make_async_copy(tokens_far.at[:, band, :], tokens.at[:, band, :], token_sems.at[number]))
        loads[-1].start()
    weights = []
    for number, piece in enumerate(pieces):
        band = pl.ds(pl.multiple_of(starts[number], 96), piece.shape[0])
        weights.append(pltpu.make_async_copy(piece, weight.at[band, :], sems.at[number]))
        weights[-1].start()
    mod_load.wait()

    for number in range(chunks):
        loads[number].wait()

        def norm_rows(step, carry, number=number):
            band = pl.ds(pl.multiple_of(number * chunk + step * step_rows, step_rows), step_rows)
            total = jnp.zeros((step_rows, 128), jnp.float32)
            for part in range(parts):
                wide = tokens[part, band, :].astype(jnp.float32)
                square = wide * wide
                for lane in range(0, depth, 128):
                    total = total + square[:, lane : lane + 128]
            scale = lax.rsqrt(jnp.sum(total, axis=-1, keepdims=True) * (1.0 / features) + EPS)
            for part in range(parts):
                span = slice(part * depth, (part + 1) * depth)
                wide = tokens[part, band, :].astype(jnp.float32)
                row = wide * scale * (1.0 + mod[0:1, span]) + mod[1:2, span]
                normed[band, span] = row.astype(jnp.bfloat16)
            return carry

        lax.fori_loop(0, chunk // step_rows, norm_rows, 0)
    for copy in weights:
        copy.wait()

    heads = q_out.shape[1] // HD

    def head_norm(part, gain):
        scale = lax.rsqrt(jnp.mean(part * part, axis=-1, keepdims=True) + EPS)
        return (part * scale * gain).astype(jnp.bfloat16)

    for head in range(heads):
        span = slice(3 * HD * head, 3 * HD * (head + 1))
        out = jnp.dot(normed[...], weight[:, span], preferred_element_type=jnp.float32)
        q_out[:, HD * head : HD * (head + 1)] = head_norm(out[:, :HD], q_gain[...])
        keys = head_norm(out[:, HD : 2 * HD], k_gain[...])
        values = out[:, 2 * HD :].astype(jnp.bfloat16)
        for item, at in ((keys, HD * head), (values, HD * (heads + head))):
            kv_out[:, at : at + HD] = item
            lo_out[:, at : at + HD] = item[: rows // 2]
            hi_out[:, at : at + HD] = item[rows // 2 :]


def key_limit(spots, frames, mask, number):
    block, segment = spots[0], spots[number]
    seen = (segment == block) | ((segment < block) & (mask[block, segment] == 1))
    return jnp.where(seen, frames[0, segment] * TPF, 0)


def attend_part(limit, first, q, kv, num, den, heads):
    rows = 256
    keys = kv.shape[0]
    column = lax.broadcasted_iota(jnp.int32, (1, keys), 1) + first
    keep = column < limit
    factor = HD ** (-0.5) * math.log2(math.e)
    for head in range(heads):
        span = slice(HD * head, HD * (head + 1))
        k = kv[:, span]
        v = kv[:, HD * (heads + head) : HD * (heads + head + 1)]
        for top in range(0, q.shape[0], rows):
            band = slice(top, top + rows)
            scores = lax.dot_general(
                q[band, span], k, (((1,), (1,)), ((), ())), preferred_element_type=jnp.float32
            )
            weights = jnp.where(keep, jnp.exp2(scores * factor), 0.0)
            total = weights[:, :128]
            for lane in range(128, keys, 128):
                total = total + weights[:, lane : lane + 128]
            den[band, span] += total
            num[band, span] += jnp.dot(weights.astype(jnp.bfloat16), v, preferred_element_type=jnp.float32)


def near_kernel(spots, frames, mask, q, own, pair, num, den):
    heads = q.shape[1] // HD
    half = q.shape[0] // 2
    num[...] = jnp.zeros_like(num)
    den[...] = jnp.zeros_like(den)
    for number, kv in ((0, own), (1, pair)):
        limit = key_limit(spots, frames, mask, number)
        for first in (0, half):
            @pl.when(limit > first)
            def _(limit=limit, first=first, kv=kv):
                attend_part(limit, first, q, kv.at[first : first + half], num, den, heads)


def far_kernel(number, finish, spots, frames, mask, q, num_in, den_in, *rest):
    heads = q.shape[1] // HD
    half = q.shape[0] // 2
    num, den = rest[-2:]
    if finish:
        lo, hi = rest[0].at[:half], rest[0].at[half:]
    else:
        lo, hi = rest[:2]
    num[...] = num_in[...]
    den[...] = den_in[...]
    limit = key_limit(spots, frames, mask, number)
    for first, kv in ((0, lo), (half, hi)):
        @pl.when(limit > first)
        def _(first=first, kv=kv):
            attend_part(limit, first, q, kv, num, den, heads)
    if finish:
        for head in range(heads):
            span = slice(HD * head, HD * (head + 1))
            total = jnp.sum(den[:, span], axis=-1, keepdims=True)
            rest[1][:, span] = (num[:, span] / total).astype(jnp.bfloat16)


def body(tokens, levels, frames, segment_mask, mod_table, w_qkv, q_gain, k_gain):
    own = tokens[0, 0]
    rows, depth = own.shape
    ring = mod_table.shape[2] // depth
    part_rows, columns = w_qkv.shape
    heads = columns // (3 * HD)
    width = heads * HD
    quarter = part_rows // XS
    half = rows // 2

    block = lax.axis_index("block")
    side, core = block // CORES, block % CORES
    x = lax.axis_index("req") // YS
    other = (1 - side) * CORES
    spots = jnp.stack([block, side * CORES + 1 - core, other + core, other + 1 - core]).astype(jnp.int32)

    whole = lax.all_gather(own, "head", axis=0, tiled=False)

    w_pair = move(w_qkv, SWAP)
    first = move(lax.dynamic_slice_in_dim(w_qkv, quarter * x, quarter), MIRROR)
    up, down = move(first, X_UP), move(first, X_DOWN)
    far_a, far_b = move(up[: quarter // 2], X_UP), move(down[quarter // 2 :], X_DOWN)
    held = [(first, 0, 0), (up, 3, 0), (down, 1, 0), (far_a, 2, 0), (far_b, 2, quarter // 2)]
    pieces, starts = [w_qkv, w_pair], [block * part_rows, (side * CORES + 1 - core) * part_rows]
    for piece, away, at in held:
        row = (x + away) % XS * quarter + at
        pieces += [piece, move(piece, SWAP)]
        starts += [(other + core) * part_rows + row, (other + 1 - core) * part_rows + row]
    starts = jnp.stack(starts).astype(jnp.int32)

    smem = pl.BlockSpec(memory_space=pltpu.SMEM)
    vmem = pl.BlockSpec(memory_space=pltpu.VMEM)
    hbm = pl.BlockSpec(memory_space=pltpu.HBM)

    def sized(limit):
        return pltpu.CompilerParams(vmem_limit_bytes=int(limit * MIB))

    chunks = 4
    queries, kv, kv_lo, kv_hi = pl.pallas_call(
        functools.partial(project_kernel, len(pieces)),
        out_shape=(
            jax.ShapeDtypeStruct((rows, width), jnp.bfloat16),
            jax.ShapeDtypeStruct((rows, 2 * width), jnp.bfloat16),
            jax.ShapeDtypeStruct((half, 2 * width), jnp.bfloat16),
            jax.ShapeDtypeStruct((half, 2 * width), jnp.bfloat16),
        ),
        in_specs=[smem] * 2 + [hbm] * 2 + [vmem] * 2 + [hbm] * len(pieces),
        out_specs=(vmem,) * 4,
        scratch_shapes=[
            pltpu.VMEM((ring, rows, depth), jnp.bfloat16),
            pltpu.VMEM(mod_table.shape[1:], jnp.float32),
            pltpu.VMEM((ring * depth, columns), jnp.bfloat16),
            pltpu.VMEM((rows, ring * depth), jnp.bfloat16),
            pltpu.SemaphoreType.DMA((chunks,)),
            pltpu.SemaphoreType.DMA,
            pltpu.SemaphoreType.DMA((len(pieces),)),
        ],
        compiler_params=sized(61.5),
        cost_estimate=pl.CostEstimate(
            flops=2 * rows * ring * depth * columns, bytes_accessed=12 * MIB, transcendentals=0
        ),
        name="project",
    )(starts, levels, whole, mod_table, q_gain[None, :], k_gain[None, :], *pieces)

    far_lo = move(kv_lo, UP_FIRST)
    far_hi = move(kv_hi, DOWN_FIRST)
    pair_kv = move(kv, SWAP)

    where = (spots, frames, segment_mask[0])
    sums = (jax.ShapeDtypeStruct((rows, width), jnp.float32),) * 2
    work = pl.CostEstimate(
        flops=8 * rows * rows * width, bytes_accessed=6 * MIB, transcendentals=2 * rows * rows * heads
    )
    num, den = pl.pallas_call(
        near_kernel,
        out_shape=sums,
        in_specs=[smem] * 3 + [vmem] * 3,
        out_specs=(vmem, vmem),
        compiler_params=sized(24),
        cost_estimate=work,
        name="near",
    )(*where, queries, kv, pair_kv)
    far_lo, far_hi, num, den = lax.optimization_barrier((far_lo, far_hi, num, den))
    far_lo = move(far_lo, UP_SECOND)
    far_hi = move(far_hi, DOWN_SECOND)
    far_kv = lax.optimization_barrier(jnp.concatenate([far_lo, far_hi]))
    far_pair = move(far_kv, SWAP)
    num, den = pl.pallas_call(
        lambda *refs: far_kernel(2, False, *refs),
        out_shape=sums,
        in_specs=[smem] * 3 + [vmem] * 5,
        out_specs=(vmem, vmem),
        compiler_params=sized(24),
        cost_estimate=work,
        name="far",
    )(*where, queries, num, den, far_lo, far_hi)
    result = pl.pallas_call(
        lambda *refs: far_kernel(3, True, *refs),
        out_shape=jax.ShapeDtypeStruct((rows, width), jnp.bfloat16),
        in_specs=[smem] * 3 + [vmem] * 4,
        out_specs=vmem,
        scratch_shapes=[pltpu.VMEM((rows, width), jnp.float32)] * 2,
        compiler_params=sized(24),
        cost_estimate=work,
        name="last",
    )(*where, queries, num, den, far_pair)
    return result.reshape(1, 1, rows, width)


def solution(mesh):
    placed = (
        P("req", "block", None, "head"),
        P("req", "block"),
        P("req", None),
        P("req", None, None),
        P(),
        P("block", "head"),
        P(),
        P(),
    )
    return jax.shard_map(
        body, mesh=mesh, in_specs=placed, out_specs=P("req", "block", None, "head"), check_vma=False
    )
```

```python
import functools
import math

import jax
import jax.numpy as jnp
from jax import lax
from jax.experimental import pallas as pl
from jax.experimental.pallas import tpu as pltpu
from jax.sharding import PartitionSpec as P

HD = 128
TPF = 64
EPS = 1e-06
MIB = 1 << 20

HALVES, CORES, XS, YS = 2, 2, 4, 4
RING_Y = HALVES * YS


def place(y, core, x):
    return ((y // YS) * CORES + core) * (XS * YS) + x * YS + y % YS


def pairs(move, keep=lambda y: True):
    out = []
    for y in range(RING_Y):
        for core in range(CORES):
            for x in range(XS):
                if keep(y):
                    out.append((place(y, core, x), place(*move(y, core, x))))
    return out


MIRROR = pairs(lambda y, core, x: (RING_Y - 1 - y, core, x))
X_UP = pairs(lambda y, core, x: (y, core, (x + 1) % XS))
X_DOWN = pairs(lambda y, core, x: (y, core, (x - 1) % XS))
SWAP = pairs(lambda y, core, x: (y, 1 - core, x))
ACROSS = pairs(lambda y, core, x: (y + YS, core, x), lambda y: y < YS)


def move(array, table):
    return lax.ppermute(array, ("block", "req"), table)


def pack_kernel(starts, *refs):
    pieces, out, sems = refs[:-2], refs[-2], refs[-1]
    copies = []
    for number, piece in enumerate(pieces):
        band = pl.ds(pl.multiple_of(starts[number], 96), piece.shape[0])
        copies.append(pltpu.make_async_copy(piece, out.at[band, :], sems.at[number]))
        copies[-1].start()
    for copy in copies:
        copy.wait()


def project_kernel(n_pieces, starts, levels, *refs):
    tokens_far, table, q_gain, k_gain = refs[:4]
    pieces = refs[4 : 4 + n_pieces]
    q_out, kv_out, tokens, mod, weight, normed, projected, token_sems, mod_sem, sems = refs[4 + n_pieces :]
    parts, rows, depth = tokens.shape
    features = parts * depth
    chunks = token_sems.shape[0]
    chunk = rows // chunks
    step_rows = 64

    mod_load = pltpu.make_async_copy(table.at[levels[0, 0]], mod, mod_sem)
    mod_load.start()
    loads = []
    for number in range(chunks):
        band = pl.ds(number * chunk, chunk)
        loads.append(pltpu.make_async_copy(tokens_far.at[:, band, :], tokens.at[:, band, :], token_sems.at[number]))
        loads[-1].start()
    weights = []
    for number, piece in enumerate(pieces):
        band = pl.ds(pl.multiple_of(starts[number], 96), piece.shape[0])
        weights.append(pltpu.make_async_copy(piece, weight.at[band, :], sems.at[number]))
        weights[-1].start()
    mod_load.wait()

    for number in range(chunks):
        loads[number].wait()

        def norm_rows(step, carry, number=number):
            band = pl.ds(pl.multiple_of(number * chunk + step * step_rows, step_rows), step_rows)
            total = jnp.zeros((step_rows, 128), jnp.float32)
            for part in range(parts):
                wide = tokens[part, band, :].astype(jnp.float32)
                square = wide * wide
                for lane in range(0, depth, 128):
                    total = total + square[:, lane : lane + 128]
            scale = lax.rsqrt(jnp.sum(total, axis=-1, keepdims=True) * (1.0 / features) + EPS)
            for part in range(parts):
                span = slice(part * depth, (part + 1) * depth)
                wide = tokens[part, band, :].astype(jnp.float32)
                row = wide * scale * (1.0 + mod[0:1, span]) + mod[1:2, span]
                normed[band, span] = row.astype(jnp.bfloat16)
            return carry

        lax.fori_loop(0, chunk // step_rows, norm_rows, 0)
    for copy in weights:
        copy.wait()

    heads = q_out.shape[1] // HD

    def head_norm(part, gain):
        scale = lax.rsqrt(jnp.mean(part * part, axis=-1, keepdims=True) + EPS)
        return (part * scale * gain).astype(jnp.bfloat16)

    part = pieces[0].shape[0]
    columns = weight.shape[1]
    for at in range(0, columns, 512):
        span = slice(at, min(at + 512, columns))
        total = jnp.dot(normed[:, :part], weight[:part, span], preferred_element_type=jnp.float32)
        for deep in range(part, features, part):
            total += jnp.dot(
                normed[:, deep : deep + part], weight[deep : deep + part, span], preferred_element_type=jnp.float32
            )
        projected[:, span] = total
    for head in range(heads):
        at = 3 * HD * head
        q_out[:, HD * head : HD * (head + 1)] = head_norm(projected[:, at : at + HD], q_gain[...])
        keys = head_norm(projected[:, at + HD : at + 2 * HD], k_gain[...])
        values = projected[:, at + 2 * HD : at + 3 * HD].astype(jnp.bfloat16)
        kv_out[:, HD * head : HD * (head + 1)] = keys
        kv_out[:, HD * (heads + head) : HD * (heads + head + 1)] = values


def key_limit(spots, frames, mask, number):
    block, segment = spots[0], spots[number]
    seen = (segment == block) | ((segment < block) & (mask[block, segment] == 1))
    return jnp.where(seen, frames[0, segment] * TPF, 0)


def attend_part(limit, first, q, kv, num, den, heads):
    rows = 256
    keys = kv.shape[0]
    column = lax.broadcasted_iota(jnp.int32, (1, keys), 1) + first
    keep = column < limit
    factor = HD ** (-0.5) * math.log2(math.e)
    for head in range(heads):
        span = slice(HD * head, HD * (head + 1))
        k = kv[:, span]
        v = kv[:, HD * (heads + head) : HD * (heads + head + 1)]
        for top in range(0, q.shape[0], rows):
            band = slice(top, top + rows)
            scores = lax.dot_general(
                q[band, span], k, (((1,), (1,)), ((), ())), preferred_element_type=jnp.float32
            )
            weights = jnp.where(keep, jnp.exp2(scores * factor), 0.0)
            total = weights[:, :128]
            for lane in range(128, keys, 128):
                total = total + weights[:, lane : lane + 128]
            den[band, span] += total
            num[band, span] += jnp.dot(weights.astype(jnp.bfloat16), v, preferred_element_type=jnp.float32)


def near_kernel(spots, frames, mask, q, own, pair, num, den):
    heads = q.shape[1] // HD
    half = q.shape[0] // 2
    num[...] = jnp.zeros_like(num)
    den[...] = jnp.zeros_like(den)
    for number, kv in ((0, own), (1, pair)):
        limit = key_limit(spots, frames, mask, number)
        for first in (0, half):
            @pl.when(limit > first)
            def _(limit=limit, first=first, kv=kv):
                attend_part(limit, first, q, kv.at[first : first + half], num, den, heads)


def far_kernel(number, finish, spots, frames, mask, q, num_in, den_in, *rest):
    heads = q.shape[1] // HD
    half = q.shape[0] // 2
    num, den = rest[-2:]
    lo, hi = rest[0].at[:half], rest[0].at[half:]
    num[...] = num_in[...]
    den[...] = den_in[...]
    limit = key_limit(spots, frames, mask, number)
    for first, kv in ((0, lo), (half, hi)):
        @pl.when(limit > first)
        def _(first=first, kv=kv):
            attend_part(limit, first, q, kv, num, den, heads)
    if finish:
        for head in range(heads):
            span = slice(HD * head, HD * (head + 1))
            total = jnp.sum(den[:, span], axis=-1, keepdims=True)
            rest[1][:, span] = (num[:, span] / total).astype(jnp.bfloat16)


def body(tokens, levels, frames, segment_mask, mod_table, w_qkv, q_gain, k_gain):
    own = tokens[0, 0]
    rows, depth = own.shape
    ring = mod_table.shape[2] // depth
    part_rows, columns = w_qkv.shape
    heads = columns // (3 * HD)
    width = heads * HD
    quarter = part_rows // XS

    block = lax.axis_index("block")
    side, core = block // CORES, block % CORES
    x = lax.axis_index("req") // YS
    other = (1 - side) * CORES
    spots = jnp.stack([block, side * CORES + 1 - core, other + core, other + 1 - core]).astype(jnp.int32)

    whole = lax.all_gather(own, "head", axis=0, tiled=False)

    piece = quarter // 2
    mine = [lax.dynamic_slice_in_dim(w_qkv, quarter * x + at, piece) for at in (0, piece)]
    first, second = (move(item, MIRROR) for item in mine)
    first, local = lax.optimization_barrier((first, w_qkv))
    w_pair = move(local, SWAP)
    first_up, first_down = move(first, X_UP), move(first, X_DOWN)
    second, first_up, first_down = lax.optimization_barrier((second, first_up, first_down))
    second_up, second_down = move(second, X_UP), move(second, X_DOWN)
    first_far, second_far = move(first_up, X_UP), move(second_down, X_DOWN)
    held = [(first, 0, 0), (first_up, 3, 0), (first_down, 1, 0), (first_far, 2, 0),
            (second, 0, 1), (second_up, 3, 1), (second_down, 1, 1), (second_far, 2, 1)]
    places = jnp.stack([(x + away) % XS * quarter + sub * piece for _, away, sub in held]).astype(jnp.int32)
    starts = [block, side * CORES + 1 - core, other + core, other + 1 - core]
    starts = jnp.stack([item * part_rows for item in starts]).astype(jnp.int32)

    smem = pl.BlockSpec(memory_space=pltpu.SMEM)
    vmem = pl.BlockSpec(memory_space=pltpu.VMEM)
    hbm = pl.BlockSpec(memory_space=pltpu.HBM)
    anywhere = pl.BlockSpec(memory_space=pl.ANY)

    def sized(limit):
        return pltpu.CompilerParams(vmem_limit_bytes=int(limit * MIB))

    w_rest = pl.pallas_call(
        pack_kernel,
        out_shape=jax.ShapeDtypeStruct(w_qkv.shape, w_qkv.dtype),
        in_specs=[smem] + [anywhere] * len(held),
        out_specs=anywhere,
        scratch_shapes=[pltpu.SemaphoreType.DMA((len(held),))],
        compiler_params=sized(2),
        cost_estimate=pl.CostEstimate(flops=0, bytes_accessed=4 * MIB, transcendentals=0),
        name="pack",
    )(places, *(item[0] for item in held))
    pieces = [w_qkv, w_pair, w_rest, move(w_rest, SWAP)]

    chunks = 4
    queries, kv = pl.pallas_call(
        functools.partial(project_kernel, len(pieces)),
        out_shape=(
            jax.ShapeDtypeStruct((rows, width), jnp.bfloat16),
            jax.ShapeDtypeStruct((rows, 2 * width), jnp.bfloat16),
        ),
        in_specs=[smem] * 2 + [hbm] * 2 + [vmem] * 2 + [hbm] * len(pieces),
        out_specs=(vmem, vmem),
        scratch_shapes=[
            pltpu.VMEM((ring, rows, depth), jnp.bfloat16),
            pltpu.VMEM(mod_table.shape[1:], jnp.float32),
            pltpu.VMEM((ring * depth, columns), jnp.bfloat16),
            pltpu.VMEM((rows, ring * depth), jnp.bfloat16),
            pltpu.VMEM((rows, columns), jnp.float32),
            pltpu.SemaphoreType.DMA((chunks,)),
            pltpu.SemaphoreType.DMA,
            pltpu.SemaphoreType.DMA((len(pieces),)),
        ],
        compiler_params=sized(61.5),
        cost_estimate=pl.CostEstimate(
            flops=2 * rows * ring * depth * columns, bytes_accessed=12 * MIB, transcendentals=0
        ),
        name="project",
    )(starts, levels, whole, mod_table, q_gain[None, :], k_gain[None, :], *pieces)

    far_kv = move(kv, ACROSS)
    pair_kv = move(kv, SWAP)

    where = (spots, frames, segment_mask[0])
    sums = (jax.ShapeDtypeStruct((rows, width), jnp.float32),) * 2
    work = pl.CostEstimate(
        flops=8 * rows * rows * width, bytes_accessed=6 * MIB, transcendentals=2 * rows * rows * heads
    )
    num, den = pl.pallas_call(
        near_kernel,
        out_shape=sums,
        in_specs=[smem] * 3 + [vmem] * 3,
        out_specs=(vmem, vmem),
        compiler_params=sized(24),
        cost_estimate=work,
        name="near",
    )(*where, queries, kv, pair_kv)
    far_kv, num, den = lax.optimization_barrier((far_kv, num, den))
    far_pair = move(far_kv, SWAP)
    num, den = pl.pallas_call(
        lambda *refs: far_kernel(2, False, *refs),
        out_shape=sums,
        in_specs=[smem] * 3 + [vmem] * 4,
        out_specs=(vmem, vmem),
        compiler_params=sized(24),
        cost_estimate=work,
        name="far",
    )(*where, queries, num, den, far_kv)
    result = pl.pallas_call(
        lambda *refs: far_kernel(3, True, *refs),
        out_shape=jax.ShapeDtypeStruct((rows, width), jnp.bfloat16),
        in_specs=[smem] * 3 + [vmem] * 4,
        out_specs=vmem,
        scratch_shapes=[pltpu.VMEM((rows, width), jnp.float32)] * 2,
        compiler_params=sized(24),
        cost_estimate=work,
        name="last",
    )(*where, queries, num, den, far_pair)
    return result.reshape(1, 1, rows, width)


def solution(mesh):
    placed = (
        P("req", "block", None, "head"),
        P("req", "block"),
        P("req", None),
        P("req", None, None),
        P(),
        P("block", "head"),
        P(),
        P(),
    )
    return jax.shard_map(
        body, mesh=mesh, in_specs=placed, out_specs=P("req", "block", None, "head"), check_vma=False
    )
```

```python
import functools
import math

import jax
import jax.numpy as jnp
from jax import lax
from jax.experimental import pallas as pl
from jax.experimental.pallas import tpu as pltpu
from jax.sharding import PartitionSpec as P

HD = 128
TPF = 64
EPS = 1e-06
MIB = 1 << 20

HALVES, CORES, XS, YS = 2, 2, 4, 4
RING_Y = HALVES * YS


def place(y, core, x):
    return ((y // YS) * CORES + core) * (XS * YS) + x * YS + y % YS


def pairs(move, keep=lambda y: True):
    out = []
    for y in range(RING_Y):
        for core in range(CORES):
            for x in range(XS):
                if keep(y):
                    out.append((place(y, core, x), place(*move(y, core, x))))
    return out


MIRROR = pairs(lambda y, core, x: (RING_Y - 1 - y, core, x))
X_UP = pairs(lambda y, core, x: (y, core, (x + 1) % XS))
X_DOWN = pairs(lambda y, core, x: (y, core, (x - 1) % XS))
SWAP = pairs(lambda y, core, x: (y, 1 - core, x))
ACROSS = pairs(lambda y, core, x: (y + YS, core, x), lambda y: y < YS)


def move(array, table):
    return lax.ppermute(array, ("block", "req"), table)


def pack_kernel(spots, *refs):
    pieces, out, sems = refs[:-2], refs[-2], refs[-1]
    copies = []
    for number, piece in enumerate(pieces):
        band = pl.ds(pl.multiple_of(spots[4 + number], 96), piece.shape[0])
        copies.append(pltpu.make_async_copy(piece, out.at[band, :], sems.at[number]))
        copies[-1].start()
    for copy in copies:
        copy.wait()


def project_kernel(n_pieces, spots, levels, *refs):
    tokens, table, q_gain, k_gain = refs[:4]
    pieces = refs[4 : 4 + n_pieces]
    q_out, kv_out, mod, weight, normed, projected, mod_sem, sems = refs[4 + n_pieces :]
    parts, rows, depth = tokens.shape
    features = parts * depth
    step_rows = 64

    mod_load = pltpu.make_async_copy(table.at[levels[0, 0]], mod, mod_sem)
    mod_load.start()
    weights = []
    for number, piece in enumerate(pieces):
        band = pl.ds(pl.multiple_of(spots[number] * piece.shape[0], 96), piece.shape[0])
        weights.append(pltpu.make_async_copy(piece, weight.at[band, :], sems.at[number]))
        weights[-1].start()
    mod_load.wait()

    def norm_rows(step, carry):
        band = pl.ds(pl.multiple_of(step * step_rows, step_rows), step_rows)
        total = jnp.zeros((step_rows, 128), jnp.float32)
        for part in range(parts):
            wide = tokens[part, band, :].astype(jnp.float32)
            square = wide * wide
            for lane in range(0, depth, 128):
                total = total + square[:, lane : lane + 128]
        scale = lax.rsqrt(jnp.sum(total, axis=-1, keepdims=True) * (1.0 / features) + EPS)
        for part in range(parts):
            span = slice(part * depth, (part + 1) * depth)
            wide = tokens[part, band, :].astype(jnp.float32)
            row = wide * scale * (1.0 + mod[0:1, span]) + mod[1:2, span]
            normed[band, span] = row.astype(jnp.bfloat16)
        return carry

    lax.fori_loop(0, rows // step_rows, norm_rows, 0)
    for copy in weights:
        copy.wait()

    heads = q_out.shape[1] // HD

    def head_norm(part, gain):
        scale = lax.rsqrt(jnp.mean(part * part, axis=-1, keepdims=True) + EPS)
        return (part * scale * gain).astype(jnp.bfloat16)

    part = pieces[0].shape[0]
    columns = weight.shape[1]
    for at in range(0, columns, 512):
        span = slice(at, min(at + 512, columns))
        total = jnp.dot(normed[:, :part], weight[:part, span], preferred_element_type=jnp.float32)
        for deep in range(part, features, part):
            total += jnp.dot(
                normed[:, deep : deep + part], weight[deep : deep + part, span], preferred_element_type=jnp.float32
            )
        projected[:, span] = total
    for head in range(heads):
        at = 3 * HD * head
        q_out[:, HD * head : HD * (head + 1)] = head_norm(projected[:, at : at + HD], q_gain[...])
        keys = head_norm(projected[:, at + HD : at + 2 * HD], k_gain[...])
        values = projected[:, at + 2 * HD : at + 3 * HD].astype(jnp.bfloat16)
        kv_out[:, HD * head : HD * (head + 1)] = keys
        kv_out[:, HD * (heads + head) : HD * (heads + head + 1)] = values


def key_limit(spots, frames, mask, number):
    block, segment = spots[0], spots[number]
    seen = (segment == block) | ((segment < block) & (mask[block, segment] == 1))
    return jnp.where(seen, frames[0, segment] * TPF, 0)


def attend_part(limit, first, q, kv, num, den, heads):
    rows = 256
    keys = kv.shape[0]
    column = lax.broadcasted_iota(jnp.int32, (1, keys), 1) + first
    keep = column < limit
    factor = HD ** (-0.5) * math.log2(math.e)
    for head in range(heads):
        span = slice(HD * head, HD * (head + 1))
        k = kv[:, span]
        v = kv[:, HD * (heads + head) : HD * (heads + head + 1)]
        for top in range(0, q.shape[0], rows):
            band = slice(top, top + rows)
            scores = lax.dot_general(
                q[band, span], k, (((1,), (1,)), ((), ())), preferred_element_type=jnp.float32
            )
            weights = jnp.where(keep, jnp.exp2(scores * factor), 0.0)
            total = weights[:, :128]
            for lane in range(128, keys, 128):
                total = total + weights[:, lane : lane + 128]
            den[band, span] += total
            num[band, span] += jnp.dot(weights.astype(jnp.bfloat16), v, preferred_element_type=jnp.float32)


def near_kernel(spots, frames, mask, q, own, pair, num, den):
    heads = q.shape[1] // HD
    half = q.shape[0] // 2
    num[...] = jnp.zeros_like(num)
    den[...] = jnp.zeros_like(den)
    for number, kv in ((0, own), (1, pair)):
        limit = key_limit(spots, frames, mask, number)
        for first in (0, half):
            @pl.when(limit > first)
            def _(limit=limit, first=first, kv=kv):
                attend_part(limit, first, q, kv.at[first : first + half], num, den, heads)


def far_kernel(number, finish, spots, frames, mask, q, num_in, den_in, *rest):
    heads = q.shape[1] // HD
    half = q.shape[0] // 2
    num, den = rest[-2:]
    lo, hi = rest[0].at[:half], rest[0].at[half:]
    num[...] = num_in[...]
    den[...] = den_in[...]
    limit = key_limit(spots, frames, mask, number)
    for first, kv in ((0, lo), (half, hi)):
        @pl.when(limit > first)
        def _(first=first, kv=kv):
            attend_part(limit, first, q, kv, num, den, heads)
    if finish:
        for head in range(heads):
            span = slice(HD * head, HD * (head + 1))
            total = jnp.sum(den[:, span], axis=-1, keepdims=True)
            rest[1][:, span] = (num[:, span] / total).astype(jnp.bfloat16)


def body(tokens, levels, frames, segment_mask, mod_table, w_qkv, q_gain, k_gain):
    own = tokens[0, 0]
    rows, depth = own.shape
    ring = mod_table.shape[2] // depth
    part_rows, columns = w_qkv.shape
    heads = columns // (3 * HD)
    width = heads * HD
    quarter = part_rows // XS

    block = lax.axis_index("block")
    side, core = block // CORES, block % CORES
    x = lax.axis_index("req") // YS
    other = (1 - side) * CORES

    whole = lax.all_gather(own, "head", axis=0, tiled=False)

    piece = quarter // 2
    mine = [lax.dynamic_slice_in_dim(w_qkv, quarter * x + at, piece) for at in (0, piece)]
    first = move(mine[0], MIRROR)
    first, later, local = lax.optimization_barrier((first, mine[1], w_qkv))
    w_pair = move(local, SWAP)
    second = move(later, MIRROR)
    first_up, first_down = move(first, X_UP), move(first, X_DOWN)
    second, first_up, first_down = lax.optimization_barrier((second, first_up, first_down))
    second_up, second_down = move(second, X_UP), move(second, X_DOWN)
    first_far, second_far = move(first_up, X_UP), move(second_down, X_DOWN)
    held = [(first, 0, 0), (first_up, 3, 0), (first_down, 1, 0), (first_far, 2, 0),
            (second, 0, 1), (second_up, 3, 1), (second_down, 1, 1), (second_far, 2, 1)]
    blocks = [block, side * CORES + 1 - core, other + core, other + 1 - core]
    places = [(x + away) % XS * quarter + sub * piece for _, away, sub in held]
    spots = jnp.stack(blocks + places).astype(jnp.int32)

    smem = pl.BlockSpec(memory_space=pltpu.SMEM)
    vmem = pl.BlockSpec(memory_space=pltpu.VMEM)
    anywhere = pl.BlockSpec(memory_space=pl.ANY)

    def sized(limit):
        return pltpu.CompilerParams(vmem_limit_bytes=int(limit * MIB))

    w_rest = pl.pallas_call(
        pack_kernel,
        out_shape=jax.ShapeDtypeStruct(w_qkv.shape, w_qkv.dtype),
        in_specs=[smem] + [anywhere] * len(held),
        out_specs=anywhere,
        scratch_shapes=[pltpu.SemaphoreType.DMA((len(held),))],
        compiler_params=sized(2),
        cost_estimate=pl.CostEstimate(flops=0, bytes_accessed=4 * MIB, transcendentals=0),
        name="pack",
    )(spots, *(item[0] for item in held))
    pieces = [w_qkv, w_pair, w_rest, move(w_rest, SWAP)]

    queries, kv = pl.pallas_call(
        functools.partial(project_kernel, len(pieces)),
        out_shape=(
            jax.ShapeDtypeStruct((rows, width), jnp.bfloat16),
            jax.ShapeDtypeStruct((rows, 2 * width), jnp.bfloat16),
        ),
        in_specs=[smem] * 2 + [vmem, anywhere, vmem, vmem] + [anywhere] * len(pieces),
        out_specs=(vmem, vmem),
        scratch_shapes=[
            pltpu.VMEM(mod_table.shape[1:], jnp.float32),
            pltpu.VMEM((ring * depth, columns), jnp.bfloat16),
            pltpu.VMEM((rows, ring * depth), jnp.bfloat16),
            pltpu.VMEM((rows, columns), jnp.float32),
            pltpu.SemaphoreType.DMA,
            pltpu.SemaphoreType.DMA((len(pieces),)),
        ],
        compiler_params=sized(40),
        cost_estimate=pl.CostEstimate(
            flops=2 * rows * ring * depth * columns, bytes_accessed=12 * MIB, transcendentals=0
        ),
        name="project",
    )(spots, levels, whole, mod_table, q_gain[None, :], k_gain[None, :], *pieces)

    far_kv = move(kv, ACROSS)
    pair_kv = move(kv, SWAP)

    where = (spots, frames, segment_mask[0])
    sums = (jax.ShapeDtypeStruct((rows, width), jnp.float32),) * 2
    work = pl.CostEstimate(
        flops=8 * rows * rows * width, bytes_accessed=6 * MIB, transcendentals=2 * rows * rows * heads
    )
    num, den = pl.pallas_call(
        near_kernel,
        out_shape=sums,
        in_specs=[smem] * 3 + [vmem] * 3,
        out_specs=(vmem, vmem),
        compiler_params=sized(24),
        cost_estimate=work,
        name="near",
    )(*where, queries, kv, pair_kv)
    far_kv, num, den = lax.optimization_barrier((far_kv, num, den))
    far_pair = move(far_kv, SWAP)
    num, den = pl.pallas_call(
        lambda *refs: far_kernel(2, False, *refs),
        out_shape=sums,
        in_specs=[smem] * 3 + [vmem] * 4,
        out_specs=(vmem, vmem),
        compiler_params=sized(24),
        cost_estimate=work,
        name="far",
    )(*where, queries, num, den, far_kv)
    result = pl.pallas_call(
        lambda *refs: far_kernel(3, True, *refs),
        out_shape=jax.ShapeDtypeStruct((rows, width), jnp.bfloat16),
        in_specs=[smem] * 3 + [vmem] * 4,
        out_specs=vmem,
        scratch_shapes=[pltpu.VMEM((rows, width), jnp.float32)] * 2,
        compiler_params=sized(24),
        cost_estimate=work,
        name="last",
    )(*where, queries, num, den, far_pair)
    return result.reshape(1, 1, rows, width)


def solution(mesh):
    placed = (
        P("req", "block", None, "head"),
        P("req", "block"),
        P("req", None),
        P("req", None, None),
        P(),
        P("block", "head"),
        P(),
        P(),
    )
    return jax.shard_map(
        body, mesh=mesh, in_specs=placed, out_specs=P("req", "block", None, "head"), check_vma=False
    )
```

```python
import functools
import math

import jax
import jax.numpy as jnp
from jax import lax
from jax.experimental import pallas as pl
from jax.experimental.pallas import tpu as pltpu
from jax.sharding import PartitionSpec as P

HD = 128
TPF = 64
EPS = 1e-06
MIB = 1 << 20

HALVES, CORES, XS, YS = 2, 2, 4, 4
RING_Y = HALVES * YS


def place(y, core, x):
    return ((y // YS) * CORES + core) * (XS * YS) + x * YS + y % YS


def pairs(move, keep=lambda y: True):
    out = []
    for y in range(RING_Y):
        for core in range(CORES):
            for x in range(XS):
                if keep(y):
                    out.append((place(y, core, x), place(*move(y, core, x))))
    return out


MIRROR = pairs(lambda y, core, x: (RING_Y - 1 - y, core, x))
X_UP = pairs(lambda y, core, x: (y, core, (x + 1) % XS))
X_DOWN = pairs(lambda y, core, x: (y, core, (x - 1) % XS))
SWAP = pairs(lambda y, core, x: (y, 1 - core, x))
ACROSS = pairs(lambda y, core, x: (y + YS, core, x), lambda y: y < YS)


def move(array, table):
    return lax.ppermute(array, ("block", "req"), table)


def pack_kernel(spots, *refs):
    pieces, out, sems = refs[:-2], refs[-2], refs[-1]
    copies = []
    for number, piece in enumerate(pieces):
        band = pl.ds(pl.multiple_of(spots[4 + number], 96), piece.shape[0])
        copies.append(pltpu.make_async_copy(piece, out.at[band, :], sems.at[number]))
        copies[-1].start()
    for copy in copies:
        copy.wait()


def project_kernel(n_pieces, spots, levels, *refs):
    tokens_far, table, q_gain, k_gain = refs[:4]
    pieces = refs[4 : 4 + n_pieces]
    q_out, kv_out, tokens, mod, weight, normed, projected, token_sems, mod_sem, sems = refs[4 + n_pieces :]
    parts, rows, depth = tokens.shape
    features = parts * depth
    chunks = token_sems.shape[0]
    chunk = rows // chunks
    step_rows = 64

    mod_load = pltpu.make_async_copy(table.at[levels[0, 0]], mod, mod_sem)
    mod_load.start()
    loads = []
    for number in range(chunks):
        band = pl.ds(number * chunk, chunk)
        loads.append(pltpu.make_async_copy(tokens_far.at[:, band, :], tokens.at[:, band, :], token_sems.at[number]))
        loads[-1].start()
    weights = []
    for number, piece in enumerate(pieces):
        band = pl.ds(pl.multiple_of(spots[number] * piece.shape[0], 96), piece.shape[0])
        weights.append(pltpu.make_async_copy(piece, weight.at[band, :], sems.at[number]))
        weights[-1].start()
    mod_load.wait()

    for number in range(chunks):
        loads[number].wait()

        def norm_rows(step, carry, number=number):
            band = pl.ds(pl.multiple_of(number * chunk + step * step_rows, step_rows), step_rows)
            total = jnp.zeros((step_rows, 128), jnp.float32)
            for part in range(parts):
                wide = tokens[part, band, :].astype(jnp.float32)
                square = wide * wide
                for lane in range(0, depth, 128):
                    total = total + square[:, lane : lane + 128]
            scale = lax.rsqrt(jnp.sum(total, axis=-1, keepdims=True) * (1.0 / features) + EPS)
            for part in range(parts):
                span = slice(part * depth, (part + 1) * depth)
                wide = tokens[part, band, :].astype(jnp.float32)
                row = wide * scale * (1.0 + mod[0:1, span]) + mod[1:2, span]
                normed[band, span] = row.astype(jnp.bfloat16)
            return carry

        lax.fori_loop(0, chunk // step_rows, norm_rows, 0)
    for copy in weights:
        copy.wait()

    heads = q_out.shape[1] // HD

    def head_norm(part, gain):
        scale = lax.rsqrt(jnp.mean(part * part, axis=-1, keepdims=True) + EPS)
        return (part * scale * gain).astype(jnp.bfloat16)

    part = pieces[0].shape[0]
    columns = weight.shape[1]
    for at in range(0, columns, 512):
        span = slice(at, min(at + 512, columns))
        total = jnp.dot(normed[:, :part], weight[:part, span], preferred_element_type=jnp.float32)
        for deep in range(part, features, part):
            total += jnp.dot(
                normed[:, deep : deep + part], weight[deep : deep + part, span], preferred_element_type=jnp.float32
            )
        projected[:, span] = total
    for head in range(heads):
        at = 3 * HD * head
        q_out[:, HD * head : HD * (head + 1)] = head_norm(projected[:, at : at + HD], q_gain[...])
        keys = head_norm(projected[:, at + HD : at + 2 * HD], k_gain[...])
        values = projected[:, at + 2 * HD : at + 3 * HD].astype(jnp.bfloat16)
        kv_out[:, HD * head : HD * (head + 1)] = keys
        kv_out[:, HD * (heads + head) : HD * (heads + head + 1)] = values


def key_limit(spots, frames, mask, number):
    block, segment = spots[0], spots[number]
    seen = (segment == block) | ((segment < block) & (mask[block, segment] == 1))
    return jnp.where(seen, frames[0, segment] * TPF, 0)


def attend_part(limit, first, q, kv, num, den, heads):
    rows = 256
    keys = kv.shape[0]
    column = lax.broadcasted_iota(jnp.int32, (1, keys), 1) + first
    keep = column < limit
    factor = HD ** (-0.5) * math.log2(math.e)
    for head in range(heads):
        span = slice(HD * head, HD * (head + 1))
        k = kv[:, span]
        v = kv[:, HD * (heads + head) : HD * (heads + head + 1)]
        for top in range(0, q.shape[0], rows):
            band = slice(top, top + rows)
            scores = lax.dot_general(
                q[band, span], k, (((1,), (1,)), ((), ())), preferred_element_type=jnp.float32
            )
            weights = jnp.where(keep, jnp.exp2(scores * factor), 0.0)
            total = weights[:, :128]
            for lane in range(128, keys, 128):
                total = total + weights[:, lane : lane + 128]
            den[band, span] += total
            num[band, span] += jnp.dot(weights.astype(jnp.bfloat16), v, preferred_element_type=jnp.float32)


def near_kernel(spots, frames, mask, q, own, pair, num, den):
    heads = q.shape[1] // HD
    half = q.shape[0] // 2
    num[...] = jnp.zeros_like(num)
    den[...] = jnp.zeros_like(den)
    for number, kv in ((0, own), (1, pair)):
        limit = key_limit(spots, frames, mask, number)
        for first in (0, half):
            @pl.when(limit > first)
            def _(limit=limit, first=first, kv=kv):
                attend_part(limit, first, q, kv.at[first : first + half], num, den, heads)


def far_kernel(number, finish, spots, frames, mask, q, num_in, den_in, *rest):
    heads = q.shape[1] // HD
    half = q.shape[0] // 2
    num, den = rest[-2:]
    lo, hi = rest[0].at[:half], rest[0].at[half:]
    num[...] = num_in[...]
    den[...] = den_in[...]
    limit = key_limit(spots, frames, mask, number)
    for first, kv in ((0, lo), (half, hi)):
        @pl.when(limit > first)
        def _(first=first, kv=kv):
            attend_part(limit, first, q, kv, num, den, heads)
    if finish:
        for head in range(heads):
            span = slice(HD * head, HD * (head + 1))
            total = jnp.sum(den[:, span], axis=-1, keepdims=True)
            rest[1][:, span] = (num[:, span] / total).astype(jnp.bfloat16)


def body(tokens, levels, frames, segment_mask, mod_table, w_qkv, q_gain, k_gain):
    own = tokens[0, 0]
    rows, depth = own.shape
    ring = mod_table.shape[2] // depth
    part_rows, columns = w_qkv.shape
    heads = columns // (3 * HD)
    width = heads * HD
    quarter = part_rows // XS

    block = lax.axis_index("block")
    side, core = block // CORES, block % CORES
    x = lax.axis_index("req") // YS
    other = (1 - side) * CORES

    whole = lax.all_gather(own, "head", axis=0, tiled=False)

    piece = quarter // 2
    mine = [lax.dynamic_slice_in_dim(w_qkv, quarter * x + at, piece) for at in (0, piece)]
    first = move(mine[0], MIRROR)
    first, later, local = lax.optimization_barrier((first, mine[1], w_qkv))
    w_pair = move(local, SWAP)
    second = move(later, MIRROR)
    first_up, first_down = move(first, X_UP), move(first, X_DOWN)
    second, first_up, first_down = lax.optimization_barrier((second, first_up, first_down))
    second_up, second_down = move(second, X_UP), move(second, X_DOWN)
    first_far, second_far = move(first_up, X_UP), move(second_down, X_DOWN)
    held = [(first, 0, 0), (first_up, 3, 0), (first_down, 1, 0), (first_far, 2, 0),
            (second, 0, 1), (second_up, 3, 1), (second_down, 1, 1), (second_far, 2, 1)]
    blocks = [block, side * CORES + 1 - core, other + core, other + 1 - core]
    places = [(x + away) % XS * quarter + sub * piece for _, away, sub in held]
    spots = jnp.stack(blocks + places).astype(jnp.int32)

    smem = pl.BlockSpec(memory_space=pltpu.SMEM)
    vmem = pl.BlockSpec(memory_space=pltpu.VMEM)
    hbm = pl.BlockSpec(memory_space=pltpu.HBM)
    anywhere = pl.BlockSpec(memory_space=pl.ANY)

    def sized(limit):
        return pltpu.CompilerParams(vmem_limit_bytes=int(limit * MIB))

    w_rest = pl.pallas_call(
        pack_kernel,
        out_shape=jax.ShapeDtypeStruct(w_qkv.shape, w_qkv.dtype),
        in_specs=[smem] + [anywhere] * len(held),
        out_specs=anywhere,
        scratch_shapes=[pltpu.SemaphoreType.DMA((len(held),))],
        compiler_params=sized(2),
        cost_estimate=pl.CostEstimate(flops=0, bytes_accessed=4 * MIB, transcendentals=0),
        name="pack",
    )(spots, *(item[0] for item in held))
    pieces = [w_qkv, w_pair, w_rest, move(w_rest, SWAP)]

    chunks = 4
    queries, kv = pl.pallas_call(
        functools.partial(project_kernel, len(pieces)),
        out_shape=(
            jax.ShapeDtypeStruct((rows, width), jnp.bfloat16),
            jax.ShapeDtypeStruct((rows, 2 * width), jnp.bfloat16),
        ),
        in_specs=[smem] * 2 + [hbm] * 2 + [vmem] * 2 + [hbm] * len(pieces),
        out_specs=(vmem, vmem),
        scratch_shapes=[
            pltpu.VMEM((ring, rows, depth), jnp.bfloat16),
            pltpu.VMEM(mod_table.shape[1:], jnp.float32),
            pltpu.VMEM((ring * depth, columns), jnp.bfloat16),
            pltpu.VMEM((rows, ring * depth), jnp.bfloat16),
            pltpu.VMEM((rows, columns), jnp.float32),
            pltpu.SemaphoreType.DMA((chunks,)),
            pltpu.SemaphoreType.DMA,
            pltpu.SemaphoreType.DMA((len(pieces),)),
        ],
        compiler_params=sized(61.5),
        cost_estimate=pl.CostEstimate(
            flops=2 * rows * ring * depth * columns, bytes_accessed=12 * MIB, transcendentals=0
        ),
        name="project",
    )(spots, levels, whole, mod_table, q_gain[None, :], k_gain[None, :], *pieces)

    far_kv = move(kv, ACROSS)
    pair_kv = move(kv, SWAP)

    where = (spots, frames, segment_mask[0])
    sums = (jax.ShapeDtypeStruct((rows, width), jnp.float32),) * 2
    work = pl.CostEstimate(
        flops=8 * rows * rows * width, bytes_accessed=6 * MIB, transcendentals=2 * rows * rows * heads
    )
    num, den = pl.pallas_call(
        near_kernel,
        out_shape=sums,
        in_specs=[smem] * 3 + [vmem] * 3,
        out_specs=(vmem, vmem),
        compiler_params=sized(24),
        cost_estimate=work,
        name="near",
    )(*where, queries, kv, pair_kv)
    far_kv, num, den = lax.optimization_barrier((far_kv, num, den))
    far_pair = move(far_kv, SWAP)
    num, den = pl.pallas_call(
        lambda *refs: far_kernel(2, False, *refs),
        out_shape=sums,
        in_specs=[smem] * 3 + [vmem] * 4,
        out_specs=(vmem, vmem),
        compiler_params=sized(24),
        cost_estimate=work,
        name="far",
    )(*where, queries, num, den, far_kv)
    result = pl.pallas_call(
        lambda *refs: far_kernel(3, True, *refs),
        out_shape=jax.ShapeDtypeStruct((rows, width), jnp.bfloat16),
        in_specs=[smem] * 3 + [vmem] * 4,
        out_specs=vmem,
        scratch_shapes=[pltpu.VMEM((rows, width), jnp.float32)] * 2,
        compiler_params=sized(24),
        cost_estimate=work,
        name="last",
    )(*where, queries, num, den, far_pair)
    return result.reshape(1, 1, rows, width)


def solution(mesh):
    placed = (
        P("req", "block", None, "head"),
        P("req", "block"),
        P("req", None),
        P("req", None, None),
        P(),
        P("block", "head"),
        P(),
        P(),
    )
    return jax.shard_map(
        body, mesh=mesh, in_specs=placed, out_specs=P("req", "block", None, "head"), check_vma=False
    )
```
